32 devices in a mesh: groups: 2 (over x), pages: 16 (over z, y, core).
Axes of the slice: x: 2, y: 2, z: 4, core: 2. Of those that a mesh axis runs over, the one named last changes fastest.
Arguments:
- queries: bfloat16 [2, 512, 8192], P(None, 'groups'), parts along dimension 1, may hold values from -14 to 14
- kv_cache: bfloat16 [256, 128, 2, 1024], P(('groups', 'pages')), parts along dimension 0, may hold values from -14 to 14
- w_out: bfloat16 [8192, 8192], P('pages'), may hold values from -0.0625 to 0.0625
- slot_page_before: int32 [256], P(('groups', 'pages')), parts along dimension 0, may hold values from -1 to 127, as said below
- slot_page_after: int32 [256], P(('groups', 'pages')), parts along dimension 0, may hold values from -1 to 127, as said below
- move_out: int32 [32, 4], P(('groups', 'pages')), parts along dimension 0, may hold values from -1 to 7, as said below
- move_in: int32 [32, 4], P(('groups', 'pages')), parts along dimension 0, may hold values from -1 to 7, as said below
- positions: int32 [2, 512], P(None, 'groups'), parts along dimension 1, may hold values from 0 to 16383, as said below
Outputs:
- attn_output: bfloat16 [2, 512, 8192], P(None, ('groups', 'pages')), parts along dimension 1
- cache_after: bfloat16 [256, 128, 2, 1024], P(('groups', 'pages')), parts along dimension 0
The draws below stay inside these ranges and needn't reach their ends.
There are 2 independent parts, one for each index of `groups`. The reference program is written for one: setup_inputs(seed, part) draws one part's arguments, and reference() takes and returns one part's arrays. A program takes and returns all parts, laid end to end along the dimension named above; an argument that names none is the same for every part. Nothing has to cross between parts.
Inputs may be any that keep to these rules, and one draw needn't show every extreme that they name: `slot_page_before`: the logical page held by each slot; -1 marks a free slot; the live pages are the last ones of the sequence, numbered consecutively up to 127, each in exactly one slot; an owner's free slots are its last ones. `slot_page_after`: pages that are not sent keep their slot, each sent page sits in the slot that move_in names at its new owner, and a slot that sent its page is free. `move_out`: entry [j, o - 1] is a slot of owner j holding a live page, sent to owner (j + o) mod 16, or -1; the slots of one row differ; an owner sends at most one page to each of its next 4 owners. `move_in`: entry [j, o - 1] is a slot of owner j that is free before the moves, or -1, which it is exactly where move_out[(j - o) mod 16, o - 1] is -1; the slots of one row differ. Each row holds 256 consecutive positions; row 1 ends at the last position of the last live page; at most 256 positions lie between the end of row 0 and the start of row 1; all lie within the live pages.
All inputs are finite; a program needn't handle non-finite values.
Results may differ from the reference program's by a relative error of at most 0.0055.
Values may be sent and summed in bfloat16 or wider, within the bound.
A program may use at most 192 MiB of HBM per device.

```python
import jax
import jax.numpy as jnp
from jax import lax

HEADS = 64
KV_HEADS = 8
HEAD_DIM = 128
D = 8192
PAGE_TOK = 128
BLOCK = 256
PAGES_DEV = 8
MOVE_WIN = 4
OWNERS = 16
SLOTS = 128


def layout_plan(seed_key):
    base_key = jax.random.fold_in(seed_key, 7001)
    subkeys = jax.random.split(base_key, 6)
    levels = jax.random.randint(subkeys[0], (OWNERS,), 0, 4)
    percent = jnp.array([10, 40, 70, 100], jnp.int32)[levels]
    rolled = jax.random.randint(subkeys[1], (OWNERS, MOVE_WIN), 0, 100)
    send_flags = (rolled < percent[:, None]).astype(jnp.int32)
    picked = jax.random.randint(subkeys[2], (2,), 0, OWNERS)
    owner_ids = jnp.arange(OWNERS, dtype=jnp.int32)[:, None]
    offset = jnp.arange(1, MOVE_WIN + 1, dtype=jnp.int32)[None, :]
    quiet_owner = (picked[0] + OWNERS // 2) % OWNERS
    send_flags = jnp.where(owner_ids == quiet_owner, 0, send_flags)
    send_flags = jnp.where(owner_ids == picked[0], 1, send_flags)
    send_flags = jnp.where(owner_ids == (picked[1] - offset) % OWNERS, 1, send_flags)
    source = ((owner_ids - offset) % OWNERS).astype(jnp.int32)
    incoming = jnp.take_along_axis(send_flags, source, axis=0)
    received = jnp.sum(incoming, axis=1).astype(jnp.int32)
    slot_ids = jnp.arange(PAGES_DEV, dtype=jnp.int32)[None, :]
    occupied = slot_ids < (PAGES_DEV - received)[:, None]
    noise_ints = jax.random.randint(subkeys[3], (OWNERS, PAGES_DEV), 0, 1 << 20)
    ranked = jnp.where(occupied, noise_ints * PAGES_DEV + slot_ids, (1 << 20) * PAGES_DEV + slot_ids)
    order_rows = jnp.argsort(ranked, axis=1).astype(jnp.int32)
    out_rank = jnp.maximum(jnp.cumsum(send_flags, axis=1) - 1, 0).astype(jnp.int32)
    move_out = jnp.where(send_flags == 1, jnp.take_along_axis(order_rows, out_rank, axis=1), -1).astype(jnp.int32)
    in_rank = (jnp.cumsum(incoming, axis=1) - 1).astype(jnp.int32)
    move_in = jnp.where(incoming == 1, (PAGES_DEV - received)[:, None] + in_rank, -1).astype(jnp.int32)
    shuffled = jax.random.permutation(subkeys[4], SLOTS).astype(jnp.int32)
    flat_occupied = occupied.reshape(SLOTS)
    order_all = jnp.argsort(jnp.where(flat_occupied, shuffled, SLOTS + shuffled))
    rank_all = jnp.argsort(order_all).astype(jnp.int32)
    live_pages = (SLOTS - jnp.sum(received)).astype(jnp.int32)
    first_page = (SLOTS - live_pages).astype(jnp.int32)
    before = jnp.where(flat_occupied, rank_all + first_page, -1).astype(jnp.int32)
    before_grid = before.reshape(OWNERS, PAGES_DEV)
    sent_slots = jnp.any(move_out[:, :, None] == slot_ids[:, None, :], axis=1)
    after_ids = jnp.where(occupied & jnp.logical_not(sent_slots), before_grid, -1)
    sender_slot = jnp.take_along_axis(move_out, source, axis=0)
    arriving = jnp.where(incoming == 1, before[source * PAGES_DEV + jnp.maximum(sender_slot, 0)], -1)
    for column in range(MOVE_WIN):
        after_ids = jnp.where(slot_ids == move_in[:, column:column + 1], arriving[:, column:column + 1], after_ids)
    last_end = SLOTS * PAGE_TOK
    gap = jax.random.randint(subkeys[5], (), 0, 2 * PAGE_TOK + 1)
    steps_in = jnp.arange(BLOCK, dtype=jnp.int32)
    row_one = last_end - BLOCK + steps_in
    row_zero = last_end - 2 * BLOCK - gap + steps_in
    positions = jnp.stack([row_zero, row_one]).astype(jnp.int32)
    return (before, after_ids.reshape(SLOTS).astype(jnp.int32), move_out, move_in, positions)


def draw_slot_page_before(key, part):
    return layout_plan(key)[0]


def draw_slot_page_after(key, part):
    return layout_plan(key)[1]


def draw_move_out(key, part):
    return layout_plan(key)[2]


def draw_move_in(key, part):
    return layout_plan(key)[3]


def draw_positions(key, part):
    return layout_plan(key)[4]


def draw_kv_cache(key, part):
    shape_all = (SLOTS, PAGE_TOK, 2, KV_HEADS * HEAD_DIM)
    sample = jax.random.normal(jax.random.fold_in(key, 7003), shape_all, jnp.float32)
    key_rows = jnp.clip(sample[:, :, 0] * 2.0, -14.0, 14.0)
    value_rows = jnp.clip(sample[:, :, 1], -6.0, 6.0)
    return jnp.stack([key_rows, value_rows], axis=2).astype(jnp.bfloat16)


def draw_queries(key, part):
    shape_all = (2, BLOCK, D)
    sample = jnp.clip(jax.random.normal(jax.random.fold_in(key, 7004), shape_all, jnp.float32), -6.0, 6.0)
    return sample.astype(jnp.bfloat16)


def level_of(key, extent, cuts, smallest, top_value):
    level, own = 1.0, jax.random.fold_in(key, 6)
    for dim, shards_of in cuts:
        draws = jnp.exp(jax.random.uniform(jax.random.fold_in(own, dim), (shards_of,), jnp.float32, smallest / len(cuts), top_value / len(cuts)))
        level = level * jnp.repeat(draws, extent[dim] // shards_of).reshape([-1 if axis == dim else 1 for axis in range(len(extent))])
    return level


def normal_values(key, dims, scale, bound, shards=(), kind=jnp.bfloat16):
    level = level_of(key, dims, shards, -0.22, 0.18) if shards else 1.0
    drawn = jax.random.normal(key, dims, jnp.float32) * scale * level
    return jnp.minimum(jnp.maximum(drawn, -bound), bound).astype(kind)


def setup_inputs(seed: int = 0, part: int = 0) -> dict:
    splits = jax.random.split(jax.random.key(seed), 9)
    part_keys = jax.random.split(jax.random.fold_in(splits[8], part), 9)
    queries = draw_queries(jax.random.fold_in(jax.random.fold_in(splits[8], part), 71), part)
    kv_cache = draw_kv_cache(jax.random.fold_in(jax.random.fold_in(splits[8], part), 71), part)
    w_out = normal_values(splits[2], (D, D), D ** -0.5, 0.0625, ((0, 16),))
    slot_page_before = draw_slot_page_before(jax.random.fold_in(jax.random.fold_in(splits[8], part), 71), part)
    slot_page_after = draw_slot_page_after(jax.random.fold_in(jax.random.fold_in(splits[8], part), 71), part)
    move_out = draw_move_out(jax.random.fold_in(jax.random.fold_in(splits[8], part), 71), part)
    move_in = draw_move_in(jax.random.fold_in(jax.random.fold_in(splits[8], part), 71), part)
    positions = draw_positions(jax.random.fold_in(jax.random.fold_in(splits[8], part), 71), part)
    return dict(queries=queries, kv_cache=kv_cache, w_out=w_out, slot_page_before=slot_page_before, slot_page_after=slot_page_after, move_out=move_out, move_in=move_in, positions=positions)


floor_score = -1e30


def group_partials(query_rows, cache_rows, slot_table, positions_row):
    key_count = PAGES_DEV * PAGE_TOK
    head_group = HEADS // KV_HEADS
    key_rows = cache_rows[:, :, 0, :].reshape(key_count, KV_HEADS, HEAD_DIM).astype(jnp.float32)
    value_rows = cache_rows[:, :, 1, :].reshape(key_count, KV_HEADS, HEAD_DIM).astype(jnp.float32)
    key_pos = (slot_table[:, None] * PAGE_TOK + jnp.arange(PAGE_TOK, dtype=jnp.int32)[None, :]).reshape(key_count)
    live_keys = jnp.repeat(slot_table >= 0, PAGE_TOK)
    query_all = query_rows.reshape(BLOCK, KV_HEADS, head_group, HEAD_DIM).astype(jnp.float32)
    scores = jnp.einsum("qhgd,khd->qhgk", query_all, key_rows) * (HEAD_DIM ** -0.5)
    visible = (live_keys[None, :] & (key_pos[None, :] <= positions_row[:, None]))[:, None, None, :]
    scores = jnp.where(visible, scores, floor_score)
    row_max = jnp.max(scores, axis=-1)
    weights = jnp.where(visible, jnp.exp(scores - row_max[..., None]), 0.0).astype(jnp.bfloat16)
    row_sum = jnp.sum(weights.astype(jnp.float32), axis=-1)
    mixed_rows = jnp.einsum("qhgk,khd->qhgd", weights.astype(jnp.float32), value_rows)
    return mixed_rows.reshape(BLOCK, HEADS, HEAD_DIM), row_max.reshape(BLOCK, HEADS), row_sum.reshape(BLOCK, HEADS)


def attend(query_rows, cache_all, slot_table, positions_row, w_out):
    grouped = cache_all.reshape(OWNERS, PAGES_DEV, PAGE_TOK, 2, KV_HEADS * HEAD_DIM)
    tables = slot_table.reshape(OWNERS, PAGES_DEV)
    part_out, part_max, part_sum = lax.map(
        lambda inputs: group_partials(query_rows, inputs[0], inputs[1], positions_row), (grouped, tables))
    overall = jnp.max(part_max, axis=0)
    factor = jnp.exp(part_max - overall[None])
    weighted = jnp.sum(factor[..., None] * part_out, axis=0)
    normalizer = jnp.sum(factor * part_sum, axis=0)
    attended = (weighted / normalizer[..., None]).reshape(BLOCK, D).astype(jnp.bfloat16)
    return jnp.dot(attended, w_out, preferred_element_type=jnp.float32).astype(jnp.bfloat16)


def migrate(kv_cache, slot_page_after, move_out, move_in):
    grouped = kv_cache.reshape(OWNERS, PAGES_DEV, PAGE_TOK, 2, KV_HEADS * HEAD_DIM)
    after_ids = slot_page_after.reshape(OWNERS, PAGES_DEV)
    arranged = jnp.where((after_ids >= 0)[:, :, None, None, None], grouped, jnp.zeros((), grouped.dtype))
    slot_ids = jnp.arange(PAGES_DEV, dtype=jnp.int32)
    for offset in range(1, MOVE_WIN + 1):
        sender = jnp.roll(grouped, offset, axis=0)
        sender_slot = jnp.maximum(jnp.roll(move_out[:, offset - 1], offset), 0).astype(jnp.int32)
        arrived = jnp.take_along_axis(sender, sender_slot[:, None, None, None, None], axis=1)
        landing = (slot_ids[None, :] == move_in[:, offset - 1][:, None])[:, :, None, None, None]
        arranged = jnp.where(landing, arrived, arranged)
    return arranged.reshape(SLOTS, PAGE_TOK, 2, KV_HEADS * HEAD_DIM)


def reference(queries, kv_cache, w_out, slot_page_before, slot_page_after, move_out, move_in, positions):
    cache_after = migrate(kv_cache, slot_page_after, move_out, move_in)
    first_out = attend(queries[0], kv_cache, slot_page_before, positions[0], w_out)
    second = attend(queries[1], cache_after, slot_page_after, positions[1], w_out)
    return jnp.stack([first_out, second]), cache_after
```

```python
import functools
import math

import jax
import jax.numpy as jnp
from jax import lax
from jax.experimental import pallas as pl
from jax.experimental.pallas import tpu as pltpu
from jax.sharding import PartitionSpec as P

HEADS = 64
KV_HEADS = 8
HEAD_DIM = 128
PAGE_TOK = 128
MOVE_WIN = 4
SUM_ROWS = 16

floor_score = -1e30


def bit_of(me, stage):
    return lax.rem(me // (1 << stage), 2)


def partner_of(me, stage):
    return me + (1 << stage) * (1 - 2 * bit_of(me, stage))


def greet_partners(me, stages):
    barrier = pltpu.get_barrier_semaphore()
    for s in range(stages):
        pl.semaphore_signal(
            barrier, inc=1, device_id={"pages": partner_of(me, s)}, device_id_type=pl.DeviceIdType.MESH
        )
    pl.semaphore_wait(barrier, stages)


def to_partner(me, stage, src, dst, send_sem, recv_sem):
    return pltpu.make_async_remote_copy(
        src_ref=src,
        dst_ref=dst,
        send_sem=send_sem,
        recv_sem=recv_sem,
        device_id={"pages": partner_of(me, stage)},
        device_id_type=pl.DeviceIdType.MESH,
    )


def halving_schedule(chunks, stages, lag, produce, start, merge):
    def step(t, carry):
        @pl.when(t < chunks)
        def _():
            produce(t)
            start(0, t)

        for s in reversed(range(stages)):
            i = t - 1 - lag * s

            @pl.when((i >= 0) & (i < chunks))
            def _():
                merge(s, i)
                if s + 1 < stages:
                    start(s + 1, i)

        return carry

    lax.fori_loop(0, chunks + 1 + lag * (stages - 1), step, 0)


def attention_kernel(n, slots, q_ref, k_ref, vt_ref, bias_ref, out_ref, *scratch):
    stages = n.bit_length() - 1
    keep, keep_l, send, send_l, recv, recv_l = (
        scratch[k * stages : (k + 1) * stages] for k in range(6)
    )
    sems = scratch[6 * stages]
    me = lax.axis_index("pages")
    own_heads = HEADS // n
    tokens = q_ref.shape[1]
    chunks = 2 * own_heads
    group = HEADS // KV_HEADS
    score_scale = HEAD_DIM ** (-0.5) * math.log2(math.e)
    greet_partners(me, stages)

    def copies(s, i):
        return (
            to_partner(me, s, send[s].at[i], recv[s].at[i], sems.at[0, s, i], sems.at[1, s, i]),
            to_partner(me, s, send_l[s].at[i], recv_l[s].at[i], sems.at[2, s, i], sems.at[3, s, i]),
        )

    def start(s, i):
        for copy in copies(s, i):
            copy.start()

    def produce(i):
        block, j = i // own_heads, lax.rem(i, own_heads)
        mine = bit_of(me, 0)
        slot = lax.rem(i, slots)

        def pair(r, carry):
            for sent in (True, False):
                owner = 2 * r + (1 - mine if sent else mine)
                head = owner * own_heads + j
                kv = head // group
                keys = k_ref[:, pl.ds(pl.multiple_of(kv * HEAD_DIM, HEAD_DIM), HEAD_DIM)]
                rows = q_ref[block, :, pl.ds(pl.multiple_of(head * HEAD_DIM, HEAD_DIM), HEAD_DIM)]
                scores = lax.dot_general(
                    keys, rows, (((1,), (1,)), ((), ())), preferred_element_type=jnp.float32
                )
                scores = scores * score_scale + bias_ref[block]
                top = jnp.max(scores, axis=0, keepdims=True)
                weights = jnp.exp2(scores - top).astype(jnp.bfloat16)
                mixed = jnp.dot(vt_ref[kv], weights, preferred_element_type=jnp.float32)
                total = mixed[HEAD_DIM : HEAD_DIM + 1]
                mixed = mixed[:HEAD_DIM] / total
                level = top + jnp.log2(total)
                if sent:
                    send[0][i, r] = mixed.astype(jnp.bfloat16)
                    send_l[0][i, pl.ds(r, 1)] = level
                else:
                    keep[0][slot, r] = mixed
                    keep_l[0][slot, pl.ds(r, 1)] = level
            return carry

        lax.fori_loop(0, n // 2, pair, 0)

    def merge(s, i):
        for copy in copies(s, i):
            copy.wait_recv()
        slot = lax.rem(i, slots)

        def merged(r):
            la, lb = keep_l[s][slot, pl.ds(r, 1)], recv_l[s][i, pl.ds(r, 1)]
            top = jnp.maximum(la, lb)
            ea, eb = jnp.exp2(la - top), jnp.exp2(lb - top)
            total = ea + eb
            mixed = keep[s][slot, r] * (ea / total) + recv[s][i, r].astype(jnp.float32) * (eb / total)
            return mixed, top + jnp.log2(total)

        if s + 1 == stages:
            mixed, _ = merged(0)
            block, j = i // own_heads, lax.rem(i, own_heads)
            out_ref[
                pl.ds(pl.multiple_of(block * tokens, tokens), tokens),
                pl.ds(pl.multiple_of(j * HEAD_DIM, HEAD_DIM), HEAD_DIM),
            ] = mixed.T.astype(jnp.bfloat16)
            return
        mine = bit_of(me, s + 1)
        for r in range(n >> (s + 2)):
            mixed, level = merged(2 * r + 1 - mine)
            send[s + 1][i, r] = mixed.astype(jnp.bfloat16)
            send_l[s + 1][i, pl.ds(r, 1)] = level
            mixed, level = merged(2 * r + mine)
            keep[s + 1][slot, r] = mixed
            keep_l[s + 1][slot, pl.ds(r, 1)] = level

    halving_schedule(chunks, stages, 1, produce, start, merge)

    def finish(i, carry):
        for s in range(stages):
            for copy in copies(s, i):
                copy.wait_send()
        return carry

    lax.fori_loop(0, chunks, finish, 0)


def project_kernel(n, width, attended_ref, w_ref, out_ref, *scratch):
    stages = n.bit_length() - 1
    keep, send, recv = (scratch[k * stages : (k + 1) * stages] for k in range(3))
    product, sems = scratch[3 * stages :]
    me = lax.axis_index("pages")
    tok_rows = out_ref.shape[1]
    block_rows = attended_ref.shape[0] // 2
    chunks = w_ref.shape[1] // width
    greet_partners(me, stages)

    def copy(s, i):
        return to_partner(me, s, send[s].at[i], recv[s].at[i], sems.at[0, s, i], sems.at[1, s, i])

    def start(s, i):
        copy(s, i).start()

    def columns(i):
        return pl.ds(pl.multiple_of(i * width, width), width)

    def produce(i):
        product[...] = jnp.dot(
            attended_ref[...], w_ref[:, columns(i)], preferred_element_type=jnp.float32
        )
        mine = bit_of(me, 0)

        def owner_rows(owner):
            first = pl.multiple_of(owner * tok_rows, tok_rows)
            return jnp.concatenate(
                [product[pl.ds(first + block * block_rows, tok_rows)] for block in range(2)], axis=0
            )

        for r in range(n // 2):
            send[0][i, r] = owner_rows(2 * r + 1 - mine).astype(jnp.bfloat16)
            keep[0][i, r] = owner_rows(2 * r + mine)

    def merge(s, i):
        copy(s, i).wait_recv()

        def merged(r):
            return keep[s][i, r] + recv[s][i, r].astype(jnp.float32)

        if s + 1 == stages:
            rows = merged(0)
            for block in range(2):
                out_ref[block, :, columns(i)] = rows[block * tok_rows : (block + 1) * tok_rows].astype(
                    jnp.bfloat16
                )
            return
        mine = bit_of(me, s + 1)
        for r in range(n >> (s + 2)):
            send[s + 1][i, r] = merged(2 * r + 1 - mine).astype(jnp.bfloat16)
            keep[s + 1][i, r] = merged(2 * r + mine)

    halving_schedule(chunks, stages, 2, produce, start, merge)

    def finish(i, carry):
        for s in range(stages):
            copy(s, i).wait_send()
        return carry

    lax.fori_loop(0, chunks, finish, 0)


def attention(queries, keys, values_t, bias, n):
    tokens = queries.shape[1]
    own_heads = HEADS // n
    stages = n.bit_length() - 1
    chunks = 2 * own_heads
    slots = 2
    parts = [n >> (s + 1) for s in range(stages)]
    rows = [max(8, part) for part in parts]
    vmem = pl.BlockSpec(memory_space=pltpu.VMEM)
    key_count = keys.shape[0]
    return pl.pallas_call(
        functools.partial(attention_kernel, n, slots),
        out_shape=jax.ShapeDtypeStruct((2 * tokens, own_heads * HEAD_DIM), jnp.bfloat16),
        in_specs=[vmem] * 4,
        out_specs=vmem,
        scratch_shapes=[pltpu.VMEM((slots, p, HEAD_DIM, tokens), jnp.float32) for p in parts]
        + [pltpu.VMEM((slots, p, tokens), jnp.float32) for p in rows]
        + [pltpu.VMEM((chunks, p, HEAD_DIM, tokens), jnp.bfloat16) for p in parts]
        + [pltpu.VMEM((chunks, p, tokens), jnp.float32) for p in rows]
        + [pltpu.VMEM((chunks, p, HEAD_DIM, tokens), jnp.bfloat16) for p in parts]
        + [pltpu.VMEM((chunks, p, tokens), jnp.float32) for p in rows]
        + [pltpu.SemaphoreType.DMA((4, stages, chunks))],
        compiler_params=pltpu.CompilerParams(
            collective_id=0, has_side_effects=True, vmem_limit_bytes=60 * 1024 * 1024
        ),
        cost_estimate=pl.CostEstimate(
            flops=4 * 2 * tokens * HEADS * HEAD_DIM * key_count,
            bytes_accessed=queries.size * 2 + key_count * KV_HEADS * HEAD_DIM * 4,
            transcendentals=2 * tokens * HEADS * key_count,
        ),
    )(queries, keys, values_t, bias)


def project(attended, w_out, n):
    rows, depth = attended.shape
    d = w_out.shape[1]
    stages = n.bit_length() - 1
    width = d // 8
    chunks = d // width
    tile = rows // n
    parts = [n >> (s + 1) for s in range(stages)]
    vmem = pl.BlockSpec(memory_space=pltpu.VMEM)
    return pl.pallas_call(
        functools.partial(project_kernel, n, width),
        out_shape=jax.ShapeDtypeStruct((2, rows // 2 // n, d), jnp.bfloat16),
        in_specs=[vmem] * 2,
        out_specs=vmem,
        scratch_shapes=[pltpu.VMEM((chunks, p, tile, width), jnp.float32) for p in parts]
        + [pltpu.VMEM((chunks, p, tile, width), jnp.bfloat16) for p in parts] * 2
        + [pltpu.VMEM((rows, width), jnp.float32), pltpu.SemaphoreType.DMA((2, stages, chunks))],
        compiler_params=pltpu.CompilerParams(
            collective_id=1, has_side_effects=True, vmem_limit_bytes=60 * 1024 * 1024
        ),
        cost_estimate=pl.CostEstimate(
            flops=2 * rows * depth * d, bytes_accessed=depth * d * 2, transcendentals=0
        ),
    )(attended, w_out)


def passed_along(block, axis, distance):
    devices = range(lax.axis_size(axis))
    route = [((i - distance) % len(devices), i) for i in devices]
    return lax.ppermute(block, axis, route)


def migrate_pages(kv_cache, slot_page_after, move_out, move_in):
    slot_ids = jnp.arange(kv_cache.shape[0], dtype=jnp.int32)
    arranged = jnp.where(
        (slot_page_after >= 0)[:, None, None, None], kv_cache, jnp.zeros((), kv_cache.dtype)
    )
    for offset in range(1, MOVE_WIN + 1):
        outgoing = lax.dynamic_index_in_dim(
            kv_cache, jnp.maximum(move_out[0, offset - 1], 0), 0, keepdims=False
        )
        arrived = passed_along(outgoing, "pages", offset)
        landing = (slot_ids == move_in[0, offset - 1])[:, None, None, None]
        arranged = jnp.where(landing, arrived[None], arranged)
    return arranged


def local(
    queries, kv_cache, w_out, slot_page_before, slot_page_after, move_out, move_in, positions
):
    n = lax.axis_size("pages")
    cache_after = migrate_pages(kv_cache, slot_page_after, move_out, move_in)
    key_count = kv_cache.shape[0] * PAGE_TOK
    width = KV_HEADS * HEAD_DIM
    keys = kv_cache[:, :, 0, :].reshape(key_count, width)
    values_t = kv_cache[:, :, 1, :].reshape(key_count, KV_HEADS, HEAD_DIM).transpose(1, 2, 0)
    values_t = jnp.concatenate(
        [values_t, jnp.ones((KV_HEADS, SUM_ROWS, key_count), jnp.bfloat16)], axis=1
    )
    key_pos = (
        slot_page_before[:, None] * PAGE_TOK + jnp.arange(PAGE_TOK, dtype=jnp.int32)[None, :]
    ).reshape(key_count)
    live = jnp.repeat(slot_page_before >= 0, PAGE_TOK)
    visible = live[None, :, None] & (key_pos[None, :, None] <= positions[:, None, :])
    bias = jnp.where(visible, 0.0, floor_score).astype(jnp.float32)
    attended = attention(queries, keys, values_t, bias, n)
    return project(attended, w_out, n), cache_after


def solution(mesh):
    in_specs = (
        P(None, "groups", None),
        P(("groups", "pages"), None, None, None),
        P("pages", None),
        P(("groups", "pages")),
        P(("groups", "pages")),
        P(("groups", "pages"), None),
        P(("groups", "pages"), None),
        P(None, "groups"),
    )
    out_specs = (P(None, ("groups", "pages"), None), P(("groups", "pages"), None, None, None))
    return jax.shard_map(local, mesh=mesh, in_specs=in_specs, out_specs=out_specs, check_vma=False)
```

```python
import functools
import math

import jax
import jax.numpy as jnp
from jax import lax
from jax.experimental import pallas as pl
from jax.experimental.pallas import tpu as pltpu
from jax.sharding import PartitionSpec as P

HEADS = 64
KV_HEADS = 8
HEAD_DIM = 128
PAGE_TOK = 128
MOVE_WIN = 4
SUM_ROWS = 16

floor_score = -1e30


def bit_of(me, stage):
    return lax.rem(me // (1 << stage), 2)


def partner_of(me, stage):
    return me + (1 << stage) * (1 - 2 * bit_of(me, stage))


def greet_partners(me, stages):
    barrier = pltpu.get_barrier_semaphore()
    for s in range(stages):
        pl.semaphore_signal(
            barrier, inc=1, device_id={"pages": partner_of(me, s)}, device_id_type=pl.DeviceIdType.MESH
        )
    pl.semaphore_wait(barrier, stages)


def to_partner(me, stage, src, dst, send_sem, recv_sem):
    return pltpu.make_async_remote_copy(
        src_ref=src,
        dst_ref=dst,
        send_sem=send_sem,
        recv_sem=recv_sem,
        device_id={"pages": partner_of(me, stage)},
        device_id_type=pl.DeviceIdType.MESH,
    )


def halving_schedule(chunks, stages, lag, produce, start, merge):
    def step(t, carry):
        @pl.when(t < chunks)
        def _():
            produce(t)
            start(0, t)

        for s in reversed(range(stages)):
            i = t - 1 - lag * s

            @pl.when((i >= 0) & (i < chunks))
            def _():
                merge(s, i)
                if s + 1 < stages:
                    start(s + 1, i)

        return carry

    lax.fori_loop(0, chunks + 1 + lag * (stages - 1), step, 0)


def attention_kernel(n, slots, q_ref, k_ref, vt_ref, bias_ref, out_ref, *scratch):
    stages = n.bit_length() - 1
    keep, keep_l, send, send_l, recv, recv_l = (
        scratch[k * stages : (k + 1) * stages] for k in range(6)
    )
    sems, sent_scores, kept_scores, top_ref = scratch[6 * stages :]
    me = lax.axis_index("pages")
    own_heads = HEADS // n
    tokens = q_ref.shape[1]
    chunks = 2 * own_heads
    pairs = n // 2
    group = HEADS // KV_HEADS
    score_scale = HEAD_DIM ** (-0.5) * math.log2(math.e)
    greet_partners(me, stages)

    def copies(s, i):
        return (
            to_partner(me, s, send[s].at[i], recv[s].at[i], sems.at[0, s, i], sems.at[1, s, i]),
            to_partner(me, s, send_l[s].at[i], recv_l[s].at[i], sems.at[2, s, i], sems.at[3, s, i]),
        )

    def start(s, i):
        for copy in copies(s, i):
            copy.start()

    mine = bit_of(me, 0)

    def score(u, sent, buffer):
        i, r = u // pairs, lax.rem(u, pairs)
        block, j = i // own_heads, lax.rem(i, own_heads)
        head = (2 * r + (1 - mine if sent else mine)) * own_heads + j
        keys = k_ref[:, pl.ds(pl.multiple_of(head // group * HEAD_DIM, HEAD_DIM), HEAD_DIM)]
        rows = q_ref[block, :, pl.ds(pl.multiple_of(head * HEAD_DIM, HEAD_DIM), HEAD_DIM)]
        scores = lax.dot_general(
            keys, rows, (((1,), (1,)), ((), ())), preferred_element_type=jnp.float32
        )
        scores = scores * score_scale + bias_ref[block]
        buffer[...] = scores
        return jnp.max(scores, axis=0, keepdims=True)

    def mix(u, sent, buffer, top):
        i, r = u // pairs, lax.rem(u, pairs)
        head = (2 * r + (1 - mine if sent else mine)) * own_heads + lax.rem(i, own_heads)
        weights = jnp.exp2(buffer[...] - top).astype(jnp.bfloat16)
        mixed = jnp.dot(vt_ref[head // group], weights, preferred_element_type=jnp.float32)
        total = mixed[HEAD_DIM : HEAD_DIM + 1]
        mixed = mixed[:HEAD_DIM] * (1.0 / total)
        level = top + jnp.log2(total)
        if sent:
            send[0][i, r] = mixed.astype(jnp.bfloat16)
            send_l[0][i, pl.ds(r, 1)] = level
        else:
            slot = lax.rem(i, slots)
            keep[0][slot, r] = mixed
            keep_l[0][slot, pl.ds(r, 1)] = level

    top_ref[...] = score(0, True, sent_scores)

    def produce(i):
        def pair(r, top_sent):
            u = i * pairs + r
            top_kept = score(u, False, kept_scores)
            mix(u, True, sent_scores, top_sent)
            top_next = score(jnp.minimum(u + 1, chunks * pairs - 1), True, sent_scores)
            mix(u, False, kept_scores, top_kept)
            return top_next

        top_ref[...] = lax.fori_loop(0, pairs, pair, top_ref[...])

    def merge(s, i):
        for copy in copies(s, i):
            copy.wait_recv()
        slot = lax.rem(i, slots)

        def merged(r):
            la, lb = keep_l[s][slot, pl.ds(r, 1)], recv_l[s][i, pl.ds(r, 1)]
            top = jnp.maximum(la, lb)
            ea, eb = jnp.exp2(la - top), jnp.exp2(lb - top)
            total = ea + eb
            mixed = keep[s][slot, r] * (ea / total) + recv[s][i, r].astype(jnp.float32) * (eb / total)
            return mixed, top + jnp.log2(total)

        if s + 1 == stages:
            mixed, _ = merged(0)
            block, j = i // own_heads, lax.rem(i, own_heads)
            out_ref[
                pl.ds(pl.multiple_of(block * tokens, tokens), tokens),
                pl.ds(pl.multiple_of(j * HEAD_DIM, HEAD_DIM), HEAD_DIM),
            ] = mixed.T.astype(jnp.bfloat16)
            return
        mine = bit_of(me, s + 1)
        for r in range(n >> (s + 2)):
            mixed, level = merged(2 * r + 1 - mine)
            send[s + 1][i, r] = mixed.astype(jnp.bfloat16)
            send_l[s + 1][i, pl.ds(r, 1)] = level
            mixed, level = merged(2 * r + mine)
            keep[s + 1][slot, r] = mixed
            keep_l[s + 1][slot, pl.ds(r, 1)] = level

    halving_schedule(chunks, stages, 1, produce, start, merge)

    def finish(i, carry):
        for s in range(stages):
            for copy in copies(s, i):
                copy.wait_send()
        return carry

    lax.fori_loop(0, chunks, finish, 0)


def project_kernel(n, width, attended_ref, w_ref, out_ref, *scratch):
    stages = n.bit_length() - 1
    keep, send, recv = (scratch[k * stages : (k + 1) * stages] for k in range(3))
    product, sems = scratch[3 * stages :]
    me = lax.axis_index("pages")
    tok_rows = out_ref.shape[1]
    block_rows = attended_ref.shape[0] // 2
    chunks = w_ref.shape[1] // width
    greet_partners(me, stages)

    def copy(s, i):
        return to_partner(me, s, send[s].at[i], recv[s].at[i], sems.at[0, s, i], sems.at[1, s, i])

    def start(s, i):
        copy(s, i).start()

    def columns(i):
        return pl.ds(pl.multiple_of(i * width, width), width)

    def produce(i):
        product[...] = jnp.dot(
            attended_ref[...], w_ref[:, columns(i)], preferred_element_type=jnp.float32
        )
        mine = bit_of(me, 0)

        def owner_rows(owner):
            first = pl.multiple_of(owner * tok_rows, tok_rows)
            return jnp.concatenate(
                [product[pl.ds(first + block * block_rows, tok_rows)] for block in range(2)], axis=0
            )

        for r in range(n // 2):
            send[0][i, r] = owner_rows(2 * r + 1 - mine).astype(jnp.bfloat16)
            keep[0][i, r] = owner_rows(2 * r + mine)

    def merge(s, i):
        copy(s, i).wait_recv()

        def merged(r):
            return keep[s][i, r] + recv[s][i, r].astype(jnp.float32)

        if s + 1 == stages:
            rows = merged(0)
            for block in range(2):
                out_ref[block, :, columns(i)] = rows[block * tok_rows : (block + 1) * tok_rows].astype(
                    jnp.bfloat16
                )
            return
        mine = bit_of(me, s + 1)
        for r in range(n >> (s + 2)):
            send[s + 1][i, r] = merged(2 * r + 1 - mine).astype(jnp.bfloat16)
            keep[s + 1][i, r] = merged(2 * r + mine)

    halving_schedule(chunks, stages, 2, produce, start, merge)

    def finish(i, carry):
        for s in range(stages):
            copy(s, i).wait_send()
        return carry

    lax.fori_loop(0, chunks, finish, 0)


def attention(queries, keys, values_t, bias, n):
    tokens = queries.shape[1]
    own_heads = HEADS // n
    stages = n.bit_length() - 1
    chunks = 2 * own_heads
    slots = 2
    parts = [n >> (s + 1) for s in range(stages)]
    rows = [max(8, part) for part in parts]
    vmem = pl.BlockSpec(memory_space=pltpu.VMEM)
    key_count = keys.shape[0]
    return pl.pallas_call(
        functools.partial(attention_kernel, n, slots),
        out_shape=jax.ShapeDtypeStruct((2 * tokens, own_heads * HEAD_DIM), jnp.bfloat16),
        in_specs=[vmem] * 4,
        out_specs=vmem,
        scratch_shapes=[pltpu.VMEM((slots, p, HEAD_DIM, tokens), jnp.float32) for p in parts]
        + [pltpu.VMEM((slots, p, tokens), jnp.float32) for p in rows]
        + [pltpu.VMEM((chunks, p, HEAD_DIM, tokens), jnp.bfloat16) for p in parts]
        + [pltpu.VMEM((chunks, p, tokens), jnp.float32) for p in rows]
        + [pltpu.VMEM((chunks, p, HEAD_DIM, tokens), jnp.bfloat16) for p in parts]
        + [pltpu.VMEM((chunks, p, tokens), jnp.float32) for p in rows]
        + [pltpu.SemaphoreType.DMA((4, stages, chunks))]
        + [pltpu.VMEM((key_count, tokens), jnp.float32)] * 2
        + [pltpu.VMEM((1, tokens), jnp.float32)],
        compiler_params=pltpu.CompilerParams(
            collective_id=0, has_side_effects=True, vmem_limit_bytes=60 * 1024 * 1024
        ),
        cost_estimate=pl.CostEstimate(
            flops=4 * 2 * tokens * HEADS * HEAD_DIM * key_count,
            bytes_accessed=queries.size * 2 + key_count * KV_HEADS * HEAD_DIM * 4,
            transcendentals=2 * tokens * HEADS * key_count,
        ),
    )(queries, keys, values_t, bias)


def project(attended, w_out, n):
    rows, depth = attended.shape
    d = w_out.shape[1]
    stages = n.bit_length() - 1
    width = d // 8
    chunks = d // width
    tile = rows // n
    parts = [n >> (s + 1) for s in range(stages)]
    vmem = pl.BlockSpec(memory_space=pltpu.VMEM)
    return pl.pallas_call(
        functools.partial(project_kernel, n, width),
        out_shape=jax.ShapeDtypeStruct((2, rows // 2 // n, d), jnp.bfloat16),
        in_specs=[vmem] * 2,
        out_specs=vmem,
        scratch_shapes=[pltpu.VMEM((chunks, p, tile, width), jnp.float32) for p in parts]
        + [pltpu.VMEM((chunks, p, tile, width), jnp.bfloat16) for p in parts] * 2
        + [pltpu.VMEM((rows, width), jnp.float32), pltpu.SemaphoreType.DMA((2, stages, chunks))],
        compiler_params=pltpu.CompilerParams(
            collective_id=1, has_side_effects=True, vmem_limit_bytes=60 * 1024 * 1024
        ),
        cost_estimate=pl.CostEstimate(
            flops=2 * rows * depth * d, bytes_accessed=depth * d * 2, transcendentals=0
        ),
    )(attended, w_out)


def passed_along(block, axis, distance):
    devices = range(lax.axis_size(axis))
    route = [((i - distance) % len(devices), i) for i in devices]
    return lax.ppermute(block, axis, route)


def migrate_pages(kv_cache, slot_page_after, move_out, move_in):
    slot_ids = jnp.arange(kv_cache.shape[0], dtype=jnp.int32)
    arranged = jnp.where(
        (slot_page_after >= 0)[:, None, None, None], kv_cache, jnp.zeros((), kv_cache.dtype)
    )
    for offset in range(1, MOVE_WIN + 1):
        outgoing = lax.dynamic_index_in_dim(
            kv_cache, jnp.maximum(move_out[0, offset - 1], 0), 0, keepdims=False
        )
        arrived = passed_along(outgoing, "pages", offset)
        landing = (slot_ids == move_in[0, offset - 1])[:, None, None, None]
        arranged = jnp.where(landing, arrived[None], arranged)
    return arranged


def local(
    queries, kv_cache, w_out, slot_page_before, slot_page_after, move_out, move_in, positions
):
    n = lax.axis_size("pages")
    cache_after = migrate_pages(kv_cache, slot_page_after, move_out, move_in)
    key_count = kv_cache.shape[0] * PAGE_TOK
    width = KV_HEADS * HEAD_DIM
    pages = kv_cache.reshape(kv_cache.shape[0], 2 * PAGE_TOK, width)
    pick = (
        jnp.arange(2 * PAGE_TOK)[None, None, :]
        == 2 * jnp.arange(PAGE_TOK)[None, :, None] + jnp.arange(2)[:, None, None]
    ).astype(jnp.bfloat16)
    keys = jnp.einsum(
        "kr,srd->skd", pick[0], pages, preferred_element_type=jnp.bfloat16
    ).reshape(key_count, width)
    values_t = jnp.einsum(
        "srd,kr->dsk", pages, pick[1], preferred_element_type=jnp.bfloat16
    ).reshape(KV_HEADS, HEAD_DIM, key_count)
    values_t = jnp.concatenate(
        [values_t, jnp.ones((KV_HEADS, SUM_ROWS, key_count), jnp.bfloat16)], axis=1
    )
    key_pos = (
        slot_page_before[:, None] * PAGE_TOK + jnp.arange(PAGE_TOK, dtype=jnp.int32)[None, :]
    ).reshape(key_count)
    live = jnp.repeat(slot_page_before >= 0, PAGE_TOK)
    visible = live[None, :, None] & (key_pos[None, :, None] <= positions[:, None, :])
    bias = jnp.where(visible, 0.0, floor_score).astype(jnp.float32)
    attended = attention(queries, keys, values_t, bias, n)
    return project(attended, w_out, n), cache_after


def solution(mesh):
    in_specs = (
        P(None, "groups", None),
        P(("groups", "pages"), None, None, None),
        P("pages", None),
        P(("groups", "pages")),
        P(("groups", "pages")),
        P(("groups", "pages"), None),
        P(("groups", "pages"), None),
        P(None, "groups"),
    )
    out_specs = (P(None, ("groups", "pages"), None), P(("groups", "pages"), None, None, None))
    return jax.shard_map(local, mesh=mesh, in_specs=in_specs, out_specs=out_specs, check_vma=False)
```

```python
import functools
import math

import jax
import jax.numpy as jnp
from jax import lax
from jax.experimental import pallas as pl
from jax.experimental.pallas import tpu as pltpu
from jax.sharding import PartitionSpec as P

HEADS = 64
KV_HEADS = 8
HEAD_DIM = 128
PAGE_TOK = 128
MOVE_WIN = 4
SUM_ROWS = 16

floor_score = -1e30


def bit_of(me, stage):
    return lax.rem(me // (1 << stage), 2)


def partner_of(me, stage):
    return me + (1 << stage) * (1 - 2 * bit_of(me, stage))


def greet_partners(me, stages):
    barrier = pltpu.get_barrier_semaphore()
    for s in range(stages):
        pl.semaphore_signal(
            barrier, inc=1, device_id={"pages": partner_of(me, s)}, device_id_type=pl.DeviceIdType.MESH
        )
    pl.semaphore_wait(barrier, stages)


def to_partner(me, stage, src, dst, send_sem, recv_sem):
    return pltpu.make_async_remote_copy(
        src_ref=src,
        dst_ref=dst,
        send_sem=send_sem,
        recv_sem=recv_sem,
        device_id={"pages": partner_of(me, stage)},
        device_id_type=pl.DeviceIdType.MESH,
    )


def halving_schedule(chunks, stages, lag, produce, start, merge):
    def step(t, carry):
        @pl.when(t < chunks)
        def _():
            produce(t)
            start(0, t)

        for s in reversed(range(stages)):
            i = t - 1 - lag * s

            @pl.when((i >= 0) & (i < chunks))
            def _():
                merge(s, i)
                if s + 1 < stages:
                    start(s + 1, i)

        return carry

    lax.fori_loop(0, chunks + 1 + lag * (stages - 1), step, 0)


def attention_kernel(n, slots, q_ref, k_ref, vt_ref, bias_ref, out_ref, *scratch):
    stages = n.bit_length() - 1
    keep, keep_l, send, send_l, recv, recv_l = (
        scratch[k * stages : (k + 1) * stages] for k in range(6)
    )
    sems, sent_scores, kept_scores, top_ref = scratch[6 * stages :]
    me = lax.axis_index("pages")
    own_heads = HEADS // n
    tokens = q_ref.shape[1]
    chunks = 2 * own_heads
    pairs = n // 2
    group = HEADS // KV_HEADS
    score_scale = HEAD_DIM ** (-0.5) * math.log2(math.e)
    greet_partners(me, stages)

    def copies(s, i):
        return (
            to_partner(me, s, send[s].at[i], recv[s].at[i], sems.at[0, s, i], sems.at[1, s, i]),
            to_partner(me, s, send_l[s].at[i], recv_l[s].at[i], sems.at[2, s, i], sems.at[3, s, i]),
        )

    def start(s, i):
        for copy in copies(s, i):
            copy.start()

    mine = bit_of(me, 0)

    def score(u, sent, buffer):
        i, r = u // pairs, lax.rem(u, pairs)
        block, j = i // own_heads, lax.rem(i, own_heads)
        head = (2 * r + (1 - mine if sent else mine)) * own_heads + j
        keys = k_ref[:, pl.ds(pl.multiple_of(head // group * HEAD_DIM, HEAD_DIM), HEAD_DIM)]
        rows = q_ref[block, :, pl.ds(pl.multiple_of(head * HEAD_DIM, HEAD_DIM), HEAD_DIM)]
        scores = lax.dot_general(
            keys, rows, (((1,), (1,)), ((), ())), preferred_element_type=jnp.float32
        )
        scores = scores * score_scale + bias_ref[block]
        buffer[...] = scores
        return jnp.max(scores, axis=0, keepdims=True)

    def mix(u, sent, buffer, top):
        i, r = u // pairs, lax.rem(u, pairs)
        head = (2 * r + (1 - mine if sent else mine)) * own_heads + lax.rem(i, own_heads)
        weights = jnp.exp2(buffer[...] - top).astype(jnp.bfloat16)
        mixed = jnp.dot(vt_ref[head // group], weights, preferred_element_type=jnp.float32)
        total = mixed[HEAD_DIM : HEAD_DIM + 1]
        mixed = mixed[:HEAD_DIM] * (1.0 / total)
        level = top + jnp.log2(total)
        if sent:
            send[0][i, r] = mixed.astype(jnp.bfloat16)
            send_l[0][i, pl.ds(r, 1)] = level
        else:
            slot = lax.rem(i, slots)
            keep[0][slot, r] = mixed
            keep_l[0][slot, pl.ds(r, 1)] = level

    top_ref[...] = score(0, True, sent_scores)

    def produce(i):
        def pair(r, top_sent):
            u = i * pairs + r
            top_kept = score(u, False, kept_scores)
            mix(u, True, sent_scores, top_sent)
            top_next = score(jnp.minimum(u + 1, chunks * pairs - 1), True, sent_scores)
            mix(u, False, kept_scores, top_kept)
            return top_next

        top_ref[...] = lax.fori_loop(0, pairs, pair, top_ref[...], unroll=2)

    def merge(s, i):
        for copy in copies(s, i):
            copy.wait_recv()
        slot = lax.rem(i, slots)

        def merged(r):
            la, lb = keep_l[s][slot, pl.ds(r, 1)], recv_l[s][i, pl.ds(r, 1)]
            top = jnp.maximum(la, lb)
            ea, eb = jnp.exp2(la - top), jnp.exp2(lb - top)
            total = ea + eb
            mixed = keep[s][slot, r] * (ea / total) + recv[s][i, r].astype(jnp.float32) * (eb / total)
            return mixed, top + jnp.log2(total)

        if s + 1 == stages:
            mixed, _ = merged(0)
            block, j = i // own_heads, lax.rem(i, own_heads)
            out_ref[
                pl.ds(pl.multiple_of(block * tokens, tokens), tokens),
                pl.ds(pl.multiple_of(j * HEAD_DIM, HEAD_DIM), HEAD_DIM),
            ] = mixed.T.astype(jnp.bfloat16)
            return
        mine = bit_of(me, s + 1)
        for r in range(n >> (s + 2)):
            mixed, level = merged(2 * r + 1 - mine)
            send[s + 1][i, r] = mixed.astype(jnp.bfloat16)
            send_l[s + 1][i, pl.ds(r, 1)] = level
            mixed, level = merged(2 * r + mine)
            keep[s + 1][slot, r] = mixed
            keep_l[s + 1][slot, pl.ds(r, 1)] = level

    halving_schedule(chunks, stages, 1, produce, start, merge)

    def finish(i, carry):
        for s in range(stages):
            for copy in copies(s, i):
                copy.wait_send()
        return carry

    lax.fori_loop(0, chunks, finish, 0)


def project_kernel(n, width, attended_ref, w_ref, out_ref, *scratch):
    stages = n.bit_length() - 1
    keep, send, recv = (scratch[k * stages : (k + 1) * stages] for k in range(3))
    product, sems = scratch[3 * stages :]
    me = lax.axis_index("pages")
    tok_rows = out_ref.shape[1]
    block_rows = attended_ref.shape[0] // 2
    chunks = w_ref.shape[1] // width
    greet_partners(me, stages)

    def copy(s, i):
        return to_partner(me, s, send[s].at[i], recv[s].at[i], sems.at[0, s, i], sems.at[1, s, i])

    def start(s, i):
        copy(s, i).start()

    def columns(i):
        return pl.ds(pl.multiple_of(i * width, width), width)

    def produce(i):
        product[...] = jnp.dot(
            attended_ref[...], w_ref[:, columns(i)], preferred_element_type=jnp.float32
        )
        mine = bit_of(me, 0)

        def owner_rows(owner):
            first = pl.multiple_of(owner * tok_rows, tok_rows)
            return jnp.concatenate(
                [product[pl.ds(first + block * block_rows, tok_rows)] for block in range(2)], axis=0
            )

        for r in range(n // 2):
            send[0][i, r] = owner_rows(2 * r + 1 - mine).astype(jnp.bfloat16)
            keep[0][i, r] = owner_rows(2 * r + mine)

    def merge(s, i):
        copy(s, i).wait_recv()

        def merged(r):
            return keep[s][i, r] + recv[s][i, r].astype(jnp.float32)

        if s + 1 == stages:
            rows = merged(0)
            for block in range(2):
                out_ref[block, :, columns(i)] = rows[block * tok_rows : (block + 1) * tok_rows].astype(
                    jnp.bfloat16
                )
            return
        mine = bit_of(me, s + 1)
        for r in range(n >> (s + 2)):
            send[s + 1][i, r] = merged(2 * r + 1 - mine).astype(jnp.bfloat16)
            keep[s + 1][i, r] = merged(2 * r + mine)

    halving_schedule(chunks, stages, 2, produce, start, merge)

    def finish(i, carry):
        for s in range(stages):
            copy(s, i).wait_send()
        return carry

    lax.fori_loop(0, chunks, finish, 0)


def attention(queries, keys, values_t, bias, n):
    tokens = queries.shape[1]
    own_heads = HEADS // n
    stages = n.bit_length() - 1
    chunks = 2 * own_heads
    slots = 2
    parts = [n >> (s + 1) for s in range(stages)]
    rows = [max(8, part) for part in parts]
    vmem = pl.BlockSpec(memory_space=pltpu.VMEM)
    key_count = keys.shape[0]
    return pl.pallas_call(
        functools.partial(attention_kernel, n, slots),
        out_shape=jax.ShapeDtypeStruct((2 * tokens, own_heads * HEAD_DIM), jnp.bfloat16),
        in_specs=[vmem] * 4,
        out_specs=vmem,
        scratch_shapes=[pltpu.VMEM((slots, p, HEAD_DIM, tokens), jnp.float32) for p in parts]
        + [pltpu.VMEM((slots, p, tokens), jnp.float32) for p in rows]
        + [pltpu.VMEM((chunks, p, HEAD_DIM, tokens), jnp.bfloat16) for p in parts]
        + [pltpu.VMEM((chunks, p, tokens), jnp.float32) for p in rows]
        + [pltpu.VMEM((chunks, p, HEAD_DIM, tokens), jnp.bfloat16) for p in parts]
        + [pltpu.VMEM((chunks, p, tokens), jnp.float32) for p in rows]
        + [pltpu.SemaphoreType.DMA((4, stages, chunks))]
        + [pltpu.VMEM((key_count, tokens), jnp.float32)] * 2
        + [pltpu.VMEM((1, tokens), jnp.float32)],
        compiler_params=pltpu.CompilerParams(
            collective_id=0, has_side_effects=True, vmem_limit_bytes=60 * 1024 * 1024
        ),
        cost_estimate=pl.CostEstimate(
            flops=4 * 2 * tokens * HEADS * HEAD_DIM * key_count,
            bytes_accessed=queries.size * 2 + key_count * KV_HEADS * HEAD_DIM * 4,
            transcendentals=2 * tokens * HEADS * key_count,
        ),
    )(queries, keys, values_t, bias)


def project(attended, w_out, n):
    rows, depth = attended.shape
    d = w_out.shape[1]
    stages = n.bit_length() - 1
    width = d // 8
    chunks = d // width
    tile = rows // n
    parts = [n >> (s + 1) for s in range(stages)]
    vmem = pl.BlockSpec(memory_space=pltpu.VMEM)
    return pl.pallas_call(
        functools.partial(project_kernel, n, width),
        out_shape=jax.ShapeDtypeStruct((2, rows // 2 // n, d), jnp.bfloat16),
        in_specs=[vmem] * 2,
        out_specs=vmem,
        scratch_shapes=[pltpu.VMEM((chunks, p, tile, width), jnp.float32) for p in parts]
        + [pltpu.VMEM((chunks, p, tile, width), jnp.bfloat16) for p in parts] * 2
        + [pltpu.VMEM((rows, width), jnp.float32), pltpu.SemaphoreType.DMA((2, stages, chunks))],
        compiler_params=pltpu.CompilerParams(
            collective_id=1, has_side_effects=True, vmem_limit_bytes=60 * 1024 * 1024
        ),
        cost_estimate=pl.CostEstimate(
            flops=2 * rows * depth * d, bytes_accessed=depth * d * 2, transcendentals=0
        ),
    )(attended, w_out)


def passed_along(block, axis, distance):
    devices = range(lax.axis_size(axis))
    route = [((i - distance) % len(devices), i) for i in devices]
    return lax.ppermute(block, axis, route)


def migrate_pages(kv_cache, slot_page_after, move_out, move_in):
    slot_ids = jnp.arange(kv_cache.shape[0], dtype=jnp.int32)
    arranged = jnp.where(
        (slot_page_after >= 0)[:, None, None, None], kv_cache, jnp.zeros((), kv_cache.dtype)
    )
    for offset in range(1, MOVE_WIN + 1):
        outgoing = lax.dynamic_index_in_dim(
            kv_cache, jnp.maximum(move_out[0, offset - 1], 0), 0, keepdims=False
        )
        arrived = passed_along(outgoing, "pages", offset)
        landing = (slot_ids == move_in[0, offset - 1])[:, None, None, None]
        arranged = jnp.where(landing, arrived[None], arranged)
    return arranged


def local(
    queries, kv_cache, w_out, slot_page_before, slot_page_after, move_out, move_in, positions
):
    n = lax.axis_size("pages")
    cache_after = migrate_pages(kv_cache, slot_page_after, move_out, move_in)
    key_count = kv_cache.shape[0] * PAGE_TOK
    width = KV_HEADS * HEAD_DIM
    pages = kv_cache.reshape(kv_cache.shape[0], 2 * PAGE_TOK, width)
    pick = (
        jnp.arange(2 * PAGE_TOK)[None, None, :]
        == 2 * jnp.arange(PAGE_TOK)[None, :, None] + jnp.arange(2)[:, None, None]
    ).astype(jnp.bfloat16)
    keys = jnp.einsum(
        "kr,srd->skd", pick[0], pages, preferred_element_type=jnp.bfloat16
    ).reshape(key_count, width)
    values_t = jnp.einsum(
        "srd,kr->dsk", pages, pick[1], preferred_element_type=jnp.bfloat16
    ).reshape(KV_HEADS, HEAD_DIM, key_count)
    values_t = jnp.concatenate(
        [values_t, jnp.ones((KV_HEADS, SUM_ROWS, key_count), jnp.bfloat16)], axis=1
    )
    key_pos = (
        slot_page_before[:, None] * PAGE_TOK + jnp.arange(PAGE_TOK, dtype=jnp.int32)[None, :]
    ).reshape(key_count)
    live = jnp.repeat(slot_page_before >= 0, PAGE_TOK)
    visible = live[None, :, None] & (key_pos[None, :, None] <= positions[:, None, :])
    bias = jnp.where(visible, 0.0, floor_score).astype(jnp.float32)
    attended = attention(queries, keys, values_t, bias, n)
    return project(attended, w_out, n), cache_after


def solution(mesh):
    in_specs = (
        P(None, "groups", None),
        P(("groups", "pages"), None, None, None),
        P("pages", None),
        P(("groups", "pages")),
        P(("groups", "pages")),
        P(("groups", "pages"), None),
        P(("groups", "pages"), None),
        P(None, "groups"),
    )
    out_specs = (P(None, ("groups", "pages"), None), P(("groups", "pages"), None, None, None))
    return jax.shard_map(local, mesh=mesh, in_specs=in_specs, out_specs=out_specs, check_vma=False)
```
